128 devices in a mesh: outer: 4 (over x_lo, core), inner: 32 (over y, x_hi, z).
Axes of the slice: x: 4 (x_hi: 2, x_lo: 2; x = x_hi * 2 + x_lo), y: 4, z: 4, core: 2. Of those that a mesh axis runs over, the one named last changes fastest.
Arguments:
- queries: bfloat16 [65536, 8, 128], P(('outer', 'inner')), may hold values from -162 to 162
- keys: bfloat16 [65536, 128], P(('outer', 'inner')), may hold values from -6 to 6
- values: bfloat16 [65536, 128], P(('outer', 'inner')), may hold values from -6 to 6
- grad_out: bfloat16 [65536, 8, 128], P(('outer', 'inner')), may hold values from -6 to 6
- doc_ids: int32 [65536], P(('outer', 'inner')), may hold values from 0 to 255, never falling along the last dimension, each value on 1 to 1536 neighbouring positions
Outputs:
- grad_queries: bfloat16 [65536, 8, 128], P(('outer', 'inner'))
- grad_keys: bfloat16 [65536, 128], P(('outer', 'inner'))
- grad_values: bfloat16 [65536, 128], P(('outer', 'inner'))
The draws below stay inside these ranges and needn't reach their ends.
Inputs may be any that keep to these rules, and one draw needn't show every extreme that they name: `doc_ids`: documents are contiguous runs in the packed order, each of 1 to 1536 tokens, one of exactly 1536.
All inputs are finite; a program needn't handle non-finite values.
Results may differ from the reference program's by a relative error of at most 0.0054.
Values may be sent and summed in bfloat16 or wider, within the bound.
A program may use at most 256 MiB of HBM per device.

```python
import math
import jax
import jax.numpy as jnp
import numpy as np
from jax import lax

HEADS = 8
HD = 128
TOK_DEV = 512
REACH = 3
DOCMAX = 1536
TOKENS = 65536
DOCS = 256


def shared_keys(key):
    return jnp.clip(jax.random.normal(key, (TOKENS, HD), jnp.float32), -6.0, 6.0)


def draw_keys(key, part):
    key_rows = shared_keys(key)
    return key_rows.astype(jnp.bfloat16)


def draw_queries(key, part):
    key = jax.random.fold_in(key, 23)
    sample = jnp.clip(jax.random.normal(key, (TOKENS, HEADS, HD), jnp.float32), -6.0, 6.0)
    return sample.astype(jnp.bfloat16)


def shard_levels(rng, shape, pieces, smallest, high):
    def one(position, blocks):
        steps = jax.random.uniform(jax.random.fold_in(jax.random.fold_in(rng, 6), position), (blocks,), jnp.float32, smallest / len(pieces), high / len(pieces))
        return jnp.repeat(jnp.exp(steps), shape[position] // blocks).reshape((-1,) + (1,) * (len(shape) - position - 1))

    gain = one(*pieces[0])
    for cut in pieces[1:]:
        gain = gain * one(*cut)
    return gain


def split_up(number_of, total, limit, slope):
    portions = [(1 << 20) // math.isqrt(standing ** slope) + 1 for standing in range(2, number_of + 1)]
    surplus, counts = total - limit - (number_of - 1), [1] * (number_of - 1)
    while surplus > 0:
        candidates = [i for i in range(number_of - 1) if counts[i] < limit]
        whole, budget = sum([portions[i] for i in candidates]), surplus
        for i in candidates:
            addition = min(limit - counts[i], max(1, budget * portions[i] // whole), surplus)
            counts[i] = counts[i] + addition
            surplus = surplus - addition
    return np.array([limit] + counts)


def ragged_sizes(own_key, number_of, total, most, lean):
    if number_of == 2:
        one = jax.random.randint(own_key, (), max(1, total - most), min(most, total - 1) + 1)
        return jnp.stack([one, total - one])
    lengths = jnp.asarray(split_up(number_of, total, most, lean), jnp.int32)
    twos = (number_of - 1) // 2
    donor, receiver = lengths[1:1 + 2 * twos:2], lengths[2:2 + 2 * twos:2]
    slack = jnp.minimum(donor - 1, most - receiver)
    passed = jax.random.randint(jax.random.fold_in(own_key, 1), (twos,), 0, 1 << 20) % (slack + 1)
    lengths = lengths.at[1:1 + 2 * twos:2].set(donor - passed).at[2:2 + 2 * twos:2].set(receiver + passed)
    return lengths[jax.random.permutation(jax.random.fold_in(own_key, 2), number_of)]


def normal_values(own_key, dims, width, bound, split=(), kind=jnp.bfloat16):
    gain = shard_levels(own_key, dims, split, -0.22, 0.18) if split else 1.0
    entries = jax.random.normal(own_key, dims, jnp.float32) * width * gain
    return jnp.minimum(jnp.maximum(entries, -bound), bound).astype(kind)


def setup_inputs(seed: int = 0) -> dict:
    streams_of = jax.random.split(jax.random.key(seed), 6)
    return {
        "queries": draw_queries(jax.random.fold_in(streams_of[5], 71), 0),
        "keys": draw_keys(jax.random.fold_in(streams_of[5], 71), 0),
        "values": normal_values(streams_of[2], (TOKENS, HD), 1.0, 6.0, ((0, 128),)),
        "grad_out": normal_values(streams_of[3], (TOKENS, HEADS, HD), 1.0, 6.0, ((0, 128),)),
        "doc_ids": jnp.searchsorted(jnp.cumsum(ragged_sizes(streams_of[4], DOCS, TOKENS, DOCMAX, 2)), jnp.arange(TOKENS), side="right").astype(jnp.int32),
    }


masked_value = -1.0e30


def reference(queries, keys, values, grad_out, doc_ids):
    tok_rows = TOK_DEV
    pad_rows = REACH * TOK_DEV
    span_rows = (REACH + 1) * TOK_DEV
    block_count = TOKENS // TOK_DEV
    scaling = HD ** -0.5
    key_pad = jnp.concatenate([jnp.zeros((pad_rows, HD), jnp.float32), keys.astype(jnp.float32)], axis=0)
    val_pad = jnp.concatenate([jnp.zeros((pad_rows, HD), jnp.float32), values.astype(jnp.float32)], axis=0)
    ids_pad = jnp.concatenate([jnp.full((pad_rows,), -1, jnp.int32), doc_ids.astype(jnp.int32)], axis=0)
    query_pos = jnp.arange(tok_rows, dtype=jnp.int32)
    key_pos = jnp.arange(span_rows, dtype=jnp.int32)
    remote_rows = (key_pos < pad_rows)[:, None]

    def round_remote(partial_sum):
        rounded = lax.optimization_barrier(partial_sum.astype(jnp.bfloat16)).astype(jnp.float32)
        return jnp.where(remote_rows, rounded, partial_sum)

    def one_block(carry, block_index):
        key_acc, val_acc = carry
        start = (block_index * tok_rows).astype(jnp.int32)
        query_rows = lax.dynamic_slice_in_dim(queries, start, tok_rows, 0).astype(jnp.float32)
        grad_rows = lax.dynamic_slice_in_dim(grad_out, start, tok_rows, 0).astype(jnp.float32)
        query_ids = lax.dynamic_slice_in_dim(doc_ids.astype(jnp.int32), start, tok_rows, 0)
        key_rows = lax.dynamic_slice_in_dim(key_pad, start, span_rows, 0)
        val_rows = lax.dynamic_slice_in_dim(val_pad, start, span_rows, 0)
        key_ids = lax.dynamic_slice_in_dim(ids_pad, start, span_rows, 0)
        allowed = (query_ids[:, None] == key_ids[None, :]) & (key_pos[None, :] <= query_pos[:, None] + pad_rows)
        scores = jnp.einsum("ihc,jc->hij", query_rows, key_rows) * scaling
        scores = jnp.where(allowed[None], scores, masked_value)
        row_max = jnp.max(scores, axis=2)
        log_norm = row_max + jnp.log(jnp.sum(jnp.exp(scores - row_max[:, :, None]), axis=2))
        probs = jnp.exp(scores - log_norm[:, :, None])
        dprob = jnp.einsum("ihc,jc->hij", grad_rows, val_rows)
        delta = jnp.sum(probs * dprob, axis=2)
        dscore = (probs * (dprob - delta[:, :, None]) * scaling).astype(jnp.bfloat16)
        dscore = lax.optimization_barrier(dscore).astype(jnp.float32)
        prob_bf = lax.optimization_barrier(probs.astype(jnp.bfloat16)).astype(jnp.float32)
        grad_val = round_remote(jnp.einsum("hij,ihc->jc", prob_bf, grad_rows))
        grad_query = jnp.einsum("hij,jc->ihc", dscore, key_rows)
        grad_key = round_remote(jnp.einsum("hij,ihc->jc", dscore, query_rows))
        key_acc = lax.dynamic_update_slice_in_dim(key_acc, lax.dynamic_slice_in_dim(key_acc, start, span_rows, 0) + grad_key, start, 0)
        val_acc = lax.dynamic_update_slice_in_dim(val_acc, lax.dynamic_slice_in_dim(val_acc, start, span_rows, 0) + grad_val, start, 0)
        return (key_acc, val_acc), grad_query.astype(jnp.bfloat16)

    start_acc = (jnp.zeros((pad_rows + TOKENS, HD), jnp.float32), jnp.zeros((pad_rows + TOKENS, HD), jnp.float32))
    (key_acc, val_acc), query_blocks = lax.scan(one_block, start_acc, jnp.arange(block_count, dtype=jnp.int32))
    grad_queries = query_blocks.reshape(TOKENS, HEADS, HD)
    return grad_queries, key_acc[pad_rows:].astype(jnp.bfloat16), val_acc[pad_rows:].astype(jnp.bfloat16)
```

```python
import functools
import math

import jax
import jax.numpy as jnp
from jax import lax
from jax.experimental import pallas as pl
from jax.experimental.pallas import tpu as pltpu
from jax.sharding import PartitionSpec as P

REACH = 3
MESH = pl.DeviceIdType.MESH
BIG = 1.0e30
LANES = 128
TILE = 128
BF = jnp.bfloat16
F32 = jnp.float32


def nn(a, b):
    return lax.dot_general(a, b, (((1,), (0,)), ((), ())), preferred_element_type=F32)


def lane_groups(width):
    return [slice(j * LANES, (j + 1) * LANES) for j in range(width // LANES)]


def id_bits(ids, place):
    bit = lax.shift_right_logical(ids, place & 7) & 1
    return jnp.where(place < 8, bit, 1 - bit)


def three_pieces(x):
    first = x.astype(BF).astype(F32)
    second = (x - first).astype(BF).astype(F32)
    return first, second, x - first - second


def kernel(
    outer,
    inner,
    q_hbm,
    k_hbm,
    v_hbm,
    g_hbm,
    ids_ref,
    dq_hbm,
    dk_ref,
    dv_ref,
    kv,
    qa,
    ga,
    qt,
    gt,
    kat,
    vat,
    m_ref,
    l_ref,
    a_ref,
    dq_acc,
    dkt,
    dvt,
    part,
    got,
    dq_bf,
    load_sem,
    store_sem,
    send_sem,
    recv_sem,
    back_send_sem,
    back_recv_sem,
):
    tokens = k_hbm.shape[0]
    rows = q_hbm.shape[0]
    heads = rows // tokens
    tile_rows = TILE * heads
    tiles = tokens // TILE
    scale = LANES**-0.5
    to_log2 = scale * math.log2(math.e)
    count = outer * inner
    me = lax.axis_index("outer") * inner + lax.axis_index("inner")

    def device(delta):
        there = lax.rem(me + delta + count, count)
        return (there // inner, lax.rem(there, inner))

    barrier = pltpu.get_barrier_semaphore()
    for d in range(1, REACH + 1):
        for delta in (d, -d):
            pl.semaphore_signal(barrier, inc=1, device_id=device(delta), device_id_type=MESH)

    loads = [
        pltpu.make_async_copy(k_hbm, kv.at[0, pl.ds(0, tokens)], load_sem.at[0]),
        pltpu.make_async_copy(v_hbm, kv.at[0, pl.ds(tokens, tokens)], load_sem.at[1]),
        pltpu.make_async_copy(q_hbm, qa.at[:, pl.ds(0, LANES)], load_sem.at[2]),
        pltpu.make_async_copy(g_hbm, ga.at[:, pl.ds(0, LANES)], load_sem.at[3]),
    ]
    for copy in loads:
        copy.start()
    groups = tokens // LANES
    id_rows = jnp.concatenate(
        [ids_ref[...].astype(F32), jnp.zeros((16 - groups, LANES), F32)], axis=0
    )
    kv[0, pl.ds(2 * tokens, 16)] = id_rows.astype(BF)
    loads[0].wait()
    loads[1].wait()
    pl.semaphore_wait(barrier, 2 * REACH)

    def forward(d):
        return pltpu.make_async_remote_copy(
            src_ref=kv.at[0],
            dst_ref=kv.at[d],
            send_sem=send_sem.at[d],
            recv_sem=recv_sem.at[d],
            device_id=device(d),
            device_id_type=MESH,
        )

    def backward(d):
        return pltpu.make_async_remote_copy(
            src_ref=part.at[d],
            dst_ref=got.at[d],
            send_sem=back_send_sem.at[d],
            recv_sem=back_recv_sem.at[d],
            device_id=device(-d),
            device_id_type=MESH,
        )

    for d in range(1, REACH + 1):
        forward(d).start()

    lane = lax.broadcasted_iota(jnp.int32, (LANES, LANES), 1)
    sub = lax.broadcasted_iota(jnp.int32, (LANES, LANES), 0)
    own_ids = ids_ref[...].astype(F32)
    for t in range(tiles):
        ids_t = jnp.transpose(jnp.broadcast_to(own_ids[t : t + 1], (LANES, LANES)))
        feature = jnp.where(lane < 16, id_bits(ids_t.astype(jnp.int32), lane), 0).astype(F32)
        spread = jnp.broadcast_to(feature[:, None, :], (LANES, heads, LANES))
        qa[pl.ds(t * tile_rows, tile_rows), LANES:] = spread.reshape(tile_rows, LANES).astype(BF)

    def prepare_keys(d):
        kat[d, :LANES] = jnp.transpose(kv[d, pl.ds(0, tokens)])
        vat[d, :LANES] = jnp.transpose(kv[d, pl.ds(tokens, tokens)])
        ids = kv[d, pl.ds(2 * tokens, 16)].astype(F32)
        for j in range(groups):
            ids_j = jnp.broadcast_to(ids[j : j + 1], (LANES, LANES)).astype(jnp.int32)
            unequal = jnp.where(id_bits(ids_j, sub) == 1, 0.0, -BIG)
            ones = jnp.where(sub < 19, 1.0, 0.0)
            kat[d, LANES:, j * LANES : (j + 1) * LANES] = jnp.where(sub < 16, unequal, ones).astype(BF)
            vat[d, LANES:, j * LANES : (j + 1) * LANES] = jnp.where(sub < 3, 1.0, 0.0).astype(BF)

    tile_token = lax.broadcasted_iota(jnp.int32, (tile_rows, LANES), 0) // heads
    tile_key = lax.broadcasted_iota(jnp.int32, (tile_rows, LANES), 1)

    def pass_one(rows_at, d, keys_at, width, first, diagonal):
        scores = nn(qa[rows_at, :], kat[d, :, keys_at])
        dprob = nn(ga[rows_at, :LANES], vat[d, :LANES, keys_at])
        pieces = [scores[:, g] for g in lane_groups(width)]
        if diagonal:
            pieces[-1] = jnp.where(tile_key <= tile_token, pieces[-1], -BIG)
        top = functools.reduce(jnp.maximum, pieces)
        if not first:
            before = m_ref[rows_at, :]
            top = jnp.maximum(top, before)
            fade = jnp.exp2((before - top) * to_log2)
        m_ref[rows_at, :] = top
        norm = None if first else l_ref[rows_at, :] * fade
        total = None if first else a_ref[rows_at, :] * fade
        for piece, g in zip(pieces, lane_groups(width)):
            e = jnp.exp2((piece - top) * to_log2)
            ed = e * dprob[:, g]
            norm = e if norm is None else norm + e
            total = ed if total is None else total + ed
        l_ref[rows_at, :] = norm
        a_ref[rows_at, :] = total

    def pass_two(rows_at, d, keys_at, width, first, diagonal):
        shifted = nn(qa[rows_at, :], kat[d, :, keys_at])
        centred = nn(ga[rows_at, :], vat[d, :, keys_at])
        probs, dscores = [], []
        for j, g in enumerate(lane_groups(width)):
            x = shifted[:, g] * to_log2
            if diagonal and j == width // LANES - 1:
                x = jnp.where(tile_key <= tile_token, x, -BIG)
            p = jnp.exp2(x)
            probs.append(p.astype(BF))
            dscores.append((p * centred[:, g] * scale).astype(BF))
        probs = jnp.concatenate(probs, axis=1) if len(probs) > 1 else probs[0]
        dscores = jnp.concatenate(dscores, axis=1) if len(dscores) > 1 else dscores[0]
        dvt[:, keys_at] += nn(gt[:, rows_at], probs)
        dkt[:, keys_at] += nn(qt[:, rows_at], dscores)
        dq = nn(dscores, kv[d, keys_at, :])
        if first:
            dq_acc[rows_at, :] = dq
        else:
            dq_acc[rows_at, :] += dq

    def tile_at(t):
        return pl.ds(t * tile_rows, tile_rows)

    def whole_block(step, d):
        def one(t, carry):
            step(pl.ds(pl.multiple_of(t * tile_rows, tile_rows), tile_rows), d, pl.ds(0, tokens), tokens, False, False)
            return carry

        lax.fori_loop(0, tiles, one, 0)

    loads[2].wait()
    loads[3].wait()
    prepare_keys(0)
    for t in range(tiles):
        pass_one(tile_at(t), 0, pl.ds(0, (t + 1) * TILE), (t + 1) * TILE, True, True)
    for t in range(tiles):
        qt[:, tile_at(t)] = jnp.transpose(qa[tile_at(t), :LANES])
        gt[:, tile_at(t)] = jnp.transpose(ga[tile_at(t), :LANES])

    def near_one(step, carry):
        d = step + 1
        forward(d).wait_recv()
        prepare_keys(d)
        whole_block(pass_one, d)
        return carry

    lax.fori_loop(0, REACH - 1, near_one, 0)
    forward(REACH).wait_recv()
    prepare_keys(REACH)
    for t in range(tiles):
        pass_one(tile_at(t), REACH, pl.ds(t * TILE, tokens - t * TILE), tokens - t * TILE, False, False)

    wide_lane = lax.broadcasted_iota(jnp.int32, (tile_rows, LANES), 1)

    def normalise(t, carry):
        at = pl.ds(pl.multiple_of(t * tile_rows, tile_rows), tile_rows)
        m = m_ref[at, :]
        top = jnp.max(m, axis=1, keepdims=True)
        weight = jnp.exp2((m - top) * to_log2)
        norm = jnp.sum(l_ref[at, :] * weight, axis=1, keepdims=True)
        total = jnp.sum(a_ref[at, :] * weight, axis=1, keepdims=True)
        shift = -(top + jnp.log2(norm) * (1.0 / to_log2))
        delta = -total / norm
        s = three_pieces(shift)
        feature = qa[at, LANES:].astype(F32)
        for j in range(3):
            feature = jnp.where(wide_lane == 16 + j, s[j], feature)
        qa[at, LANES:] = feature.astype(BF)
        s = three_pieces(delta)
        feature = jnp.where(wide_lane == 0, s[0], jnp.where(wide_lane == 1, s[1], jnp.where(wide_lane == 2, s[2], 0.0)))
        ga[at, LANES:] = feature.astype(BF)
        return carry

    lax.fori_loop(0, tiles, normalise, 0)

    def clear():
        dkt[...] = jnp.zeros_like(dkt)
        dvt[...] = jnp.zeros_like(dvt)

    def send_parts(d):
        part[d, :LANES] = dkt[...].astype(BF)
        part[d, LANES:] = dvt[...].astype(BF)
        backward(d).start()

    clear()
    for t in range(tiles):
        pass_two(tile_at(t), REACH, pl.ds(t * TILE, tokens - t * TILE), tokens - t * TILE, True, False)
    send_parts(REACH)

    def near_two(step, carry):
        d = REACH - 1 - step
        clear()
        whole_block(pass_two, d)
        send_parts(d)
        return carry

    lax.fori_loop(0, REACH - 1, near_two, 0)
    clear()
    stores = []
    for t in range(tiles):
        pass_two(tile_at(t), 0, pl.ds(0, (t + 1) * TILE), (t + 1) * TILE, False, True)
        dq_bf[tile_at(t), :] = dq_acc[tile_at(t), :].astype(BF)
        stores.append(pltpu.make_async_copy(dq_bf.at[tile_at(t)], dq_hbm.at[tile_at(t)], store_sem.at[t]))
        stores[-1].start()

    key_total, val_total = dkt[...], dvt[...]
    for d in range(REACH, 0, -1):
        backward(d).wait_recv()
        key_total = key_total + got[d, :LANES].astype(F32)
        val_total = val_total + got[d, LANES:].astype(F32)
    dk_ref[...] = jnp.transpose(key_total).astype(BF)
    dv_ref[...] = jnp.transpose(val_total).astype(BF)
    for copy in stores:
        copy.wait()
    for d in range(1, REACH + 1):
        forward(d).wait_send()
        backward(d).wait_send()


def local(outer, inner, queries, keys, values, grad_out, doc_ids):
    tokens, heads, width = queries.shape
    rows = tokens * heads
    vmem = pltpu.VMEM
    slots = REACH + 1
    grad_queries, grad_keys, grad_values = pl.pallas_call(
        functools.partial(kernel, outer, inner),
        out_shape=(
            jax.ShapeDtypeStruct((rows, width), BF),
            jax.ShapeDtypeStruct((tokens, width), BF),
            jax.ShapeDtypeStruct((tokens, width), BF),
        ),
        in_specs=[pl.BlockSpec(memory_space=pl.ANY)] * 4 + [pl.BlockSpec(memory_space=vmem)],
        out_specs=(
            pl.BlockSpec(memory_space=pl.ANY),
            pl.BlockSpec(memory_space=vmem),
            pl.BlockSpec(memory_space=vmem),
        ),
        scratch_shapes=[
            vmem((slots, 2 * tokens + 16, width), BF),
            vmem((rows, 2 * width), BF),
            vmem((rows, 2 * width), BF),
            vmem((width, rows), BF),
            vmem((width, rows), BF),
            vmem((slots, 2 * width, tokens), BF),
            vmem((slots, 2 * width, tokens), BF),
            vmem((rows, width), F32),
            vmem((rows, width), F32),
            vmem((rows, width), F32),
            vmem((rows, width), F32),
            vmem((width, tokens), F32),
            vmem((width, tokens), F32),
            vmem((slots, 2 * width, tokens), BF),
            vmem((slots, 2 * width, tokens), BF),
            vmem((rows, width), BF),
            pltpu.SemaphoreType.DMA((4,)),
            pltpu.SemaphoreType.DMA((tokens // TILE,)),
            pltpu.SemaphoreType.DMA((slots,)),
            pltpu.SemaphoreType.DMA((slots,)),
            pltpu.SemaphoreType.DMA((slots,)),
            pltpu.SemaphoreType.DMA((slots,)),
        ],
        compiler_params=pltpu.CompilerParams(
            collective_id=0, has_side_effects=True, vmem_limit_bytes=56 * 2**20
        ),
        cost_estimate=pl.CostEstimate(
            flops=14 * rows * 1664 * width, bytes_accessed=8 * rows * width, transcendentals=2 * rows * 1664
        ),
    )(
        queries.reshape(rows, width),
        keys,
        values,
        grad_out.reshape(rows, width),
        doc_ids.reshape(tokens // LANES, LANES),
    )
    return grad_queries.reshape(queries.shape), grad_keys, grad_values


def solution(mesh):
    both = ("outer", "inner")
    return jax.shard_map(
        functools.partial(local, mesh.shape["outer"], mesh.shape["inner"]),
        mesh=mesh,
        in_specs=(P(both, None, None), P(both, None), P(both, None), P(both, None, None), P(both)),
        out_specs=(P(both, None, None), P(both, None), P(both, None)),
        check_vma=False,
    )
```

```python
import functools
import math

import jax
import jax.numpy as jnp
from jax import lax
from jax.experimental import pallas as pl
from jax.experimental.pallas import tpu as pltpu
from jax.sharding import PartitionSpec as P

REACH = 3
MESH = pl.DeviceIdType.MESH
BIG = 1.0e30
LANES = 128
TILE = 128
SEND_ORDER = ((0, 1), (0, 2), (0, 3), (1, 1), (1, 2), (1, 3))
BF = jnp.bfloat16
F32 = jnp.float32


def nn(a, b):
    return lax.dot_general(a, b, (((1,), (0,)), ((), ())), preferred_element_type=F32)


def lane_groups(width):
    return [slice(j * LANES, (j + 1) * LANES) for j in range(width // LANES)]


def id_bits(ids, place):
    bit = lax.shift_right_logical(ids, place & 7) & 1
    return jnp.where(place < 8, bit, 1 - bit)


def three_pieces(x):
    first = x.astype(BF).astype(F32)
    second = (x - first).astype(BF).astype(F32)
    return first, second, x - first - second


def kernel(
    outer,
    inner,
    q_hbm,
    k_hbm,
    v_hbm,
    g_hbm,
    ids_ref,
    dq_hbm,
    dk_ref,
    dv_ref,
    kv,
    qa,
    ga,
    qt,
    gt,
    kat,
    vat,
    s_mid,
    s_edge,
    m_ref,
    l_ref,
    dq_acc,
    dkt,
    dvt,
    part,
    got,
    dq_bf,
    load_sem,
    store_sem,
    send_sem,
    recv_sem,
    back_send_sem,
    back_recv_sem,
):
    tokens = k_hbm.shape[0]
    rows = q_hbm.shape[0]
    heads = rows // tokens
    tile_rows = TILE * heads
    tiles = tokens // TILE
    scale = LANES**-0.5
    to_log2 = scale * math.log2(math.e)
    count = outer * inner
    me = lax.axis_index("outer") * inner + lax.axis_index("inner")

    def device(delta):
        there = lax.rem(me + delta + count, count)
        return (there // inner, lax.rem(there, inner))

    barrier = pltpu.get_barrier_semaphore()
    for d in range(1, REACH + 1):
        for delta in (d, -d):
            pl.semaphore_signal(barrier, inc=1, device_id=device(delta), device_id_type=MESH)

    loads = [
        pltpu.make_async_copy(k_hbm, kv.at[0, pl.ds(tokens, tokens)], load_sem.at[0]),
        pltpu.make_async_copy(v_hbm, kv.at[0, pl.ds(0, tokens)], load_sem.at[1]),
        pltpu.make_async_copy(q_hbm, qa.at[:, pl.ds(0, LANES)], load_sem.at[2]),
        pltpu.make_async_copy(g_hbm, ga.at[:, pl.ds(0, LANES)], load_sem.at[3]),
    ]
    for copy in loads:
        copy.start()
    groups = tokens // LANES
    id_rows = jnp.concatenate(
        [ids_ref[...].astype(F32), jnp.zeros((16 - groups, LANES), F32)], axis=0
    )
    kv[0, pl.ds(2 * tokens, 16)] = id_rows.astype(BF)
    loads[0].wait()
    loads[1].wait()
    pl.semaphore_wait(barrier, 2 * REACH)

    def forward(half, d):
        at = pl.ds(tokens, tokens + 16) if half == 0 else pl.ds(0, tokens)
        return pltpu.make_async_remote_copy(
            src_ref=kv.at[0, at],
            dst_ref=kv.at[d, at],
            send_sem=send_sem.at[half, d],
            recv_sem=recv_sem.at[half, d],
            device_id=device(d),
            device_id_type=MESH,
        )

    def backward(half, d):
        return pltpu.make_async_remote_copy(
            src_ref=part.at[half, d],
            dst_ref=got.at[half, d],
            send_sem=back_send_sem.at[half, d],
            recv_sem=back_recv_sem.at[half, d],
            device_id=device(-d),
            device_id_type=MESH,
        )

    for half, d in SEND_ORDER:
        forward(half, d).start()

    lane = lax.broadcasted_iota(jnp.int32, (LANES, LANES), 1)
    sub = lax.broadcasted_iota(jnp.int32, (LANES, LANES), 0)
    own_ids = ids_ref[...].astype(F32)
    for t in range(tiles):
        ids_t = jnp.transpose(jnp.broadcast_to(own_ids[t : t + 1], (LANES, LANES)))
        feature = jnp.where(lane < 16, id_bits(ids_t.astype(jnp.int32), lane), 0).astype(F32)
        spread = jnp.broadcast_to(feature[:, None, :], (LANES, heads, LANES))
        qa[pl.ds(t * tile_rows, tile_rows), LANES:] = spread.reshape(tile_rows, LANES).astype(BF)

    def prepare_keys(d):
        kat[d, :LANES] = jnp.transpose(kv[d, pl.ds(tokens, tokens)])
        ids = kv[d, pl.ds(2 * tokens, 16)].astype(F32)
        for j in range(groups):
            ids_j = jnp.broadcast_to(ids[j : j + 1], (LANES, LANES)).astype(jnp.int32)
            unequal = jnp.where((id_bits(ids_j, sub) == 0) & (sub < 16), -BIG, 0.0)
            kat[d, LANES:, j * LANES : (j + 1) * LANES] = unequal.astype(BF)

    def prepare_values(d):
        vat[d, :LANES] = jnp.transpose(kv[d, pl.ds(0, tokens)])
        ones = jnp.where(lax.broadcasted_iota(jnp.int32, (LANES, tokens), 0) < 3, 1.0, 0.0)
        vat[d, LANES:] = ones.astype(BF)

    tile_token = lax.broadcasted_iota(jnp.int32, (tile_rows, LANES), 0) // heads
    tile_key = lax.broadcasted_iota(jnp.int32, (tile_rows, LANES), 1)

    def tile_at(t):
        return pl.ds(t * tile_rows, tile_rows)

    def keys_of(d, t):
        if d == 0:
            return 0, (t + 1) * TILE
        if d == REACH:
            return t * TILE, tokens - t * TILE
        return 0, tokens

    def stored(d, t):
        if d == 0:
            return s_edge.at[tile_at(t), pl.ds(0, (t + 1) * TILE)]
        if d == REACH:
            return s_edge.at[tile_at(t), pl.ds((t + 1) * TILE, tokens - t * TILE)]
        return s_mid.at[d - 1, tile_at(t)]

    def score_tile(d, t):
        rows_at = tile_at(t)
        start, width = keys_of(d, t)
        scores = nn(qa[rows_at, :], kat[d, :, pl.ds(start, width)])
        pieces = [scores[:, g] for g in lane_groups(width)]
        if d == 0:
            pieces[-1] = jnp.where(tile_key <= tile_token, pieces[-1], -BIG)
        top = functools.reduce(jnp.maximum, pieces)
        norm = None
        if d > 0:
            before = m_ref[rows_at, :]
            top = jnp.maximum(top, before)
            norm = l_ref[rows_at, :] * jnp.exp2((before - top) * to_log2)
        m_ref[rows_at, :] = top
        place = stored(d, t)
        for piece, g in zip(pieces, lane_groups(width)):
            place[:, g] = piece
            e = jnp.exp2((piece - top) * to_log2)
            norm = e if norm is None else norm + e
        l_ref[rows_at, :] = norm

    def log_norm_tile(t):
        rows_at = tile_at(t)
        m = m_ref[rows_at, :]
        top = jnp.max(m, axis=1, keepdims=True)
        norm = jnp.sum(l_ref[rows_at, :] * jnp.exp2((m - top) * to_log2), axis=1, keepdims=True)
        m_ref[rows_at, :] = jnp.broadcast_to(top * to_log2 + jnp.log2(norm), (tile_rows, LANES))

    def value_tile(d, t):
        rows_at = tile_at(t)
        start, width = keys_of(d, t)
        log_norm = m_ref[rows_at, :]
        place = stored(d, t)
        probs = []
        for g in lane_groups(width):
            p = jnp.exp2(place[:, g] * to_log2 - log_norm)
            place[:, g] = p
            probs.append(p.astype(BF))
        probs = jnp.concatenate(probs, axis=1) if len(probs) > 1 else probs[0]
        dvt[:, pl.ds(start, width)] += nn(gt[:, rows_at], probs)

    def delta_tile(d, t):
        rows_at = tile_at(t)
        start, width = keys_of(d, t)
        dprob = nn(ga[rows_at, :LANES], vat[d, :LANES, pl.ds(start, width)])
        place = stored(d, t)
        total = None if d == 0 else l_ref[rows_at, :]
        for g in lane_groups(width):
            pd = place[:, g] * dprob[:, g]
            total = pd if total is None else total + pd
        l_ref[rows_at, :] = total

    def delta_feature_tile(t):
        rows_at = tile_at(t)
        pieces = three_pieces(-jnp.sum(l_ref[rows_at, :], axis=1, keepdims=True))
        feature = jnp.zeros((tile_rows, LANES), F32)
        for j, piece in enumerate(pieces):
            feature = jnp.where(tile_key == j, piece, feature)
        ga[rows_at, LANES:] = feature.astype(BF)

    def key_tile(d, t):
        rows_at = tile_at(t)
        start, width = keys_of(d, t)
        centred = nn(ga[rows_at, :], vat[d, :, pl.ds(start, width)])
        place = stored(d, t)
        dscores = [(place[:, g] * centred[:, g] * scale).astype(BF) for g in lane_groups(width)]
        dscores = jnp.concatenate(dscores, axis=1) if len(dscores) > 1 else dscores[0]
        dkt[:, pl.ds(start, width)] += nn(qt[:, rows_at], dscores)
        dq = nn(dscores, kv[d, pl.ds(tokens + start, width), :])
        if d == REACH:
            dq_acc[rows_at, :] = dq
        elif d > 0:
            dq_acc[rows_at, :] += dq
        else:
            dq_bf[rows_at, :] = (dq_acc[rows_at, :] + dq).astype(BF)

    loads[2].wait()
    loads[3].wait()
    prepare_keys(0)
    prepare_values(0)
    for t in range(tiles):
        score_tile(0, t)
    for t in range(tiles):
        qt[:, tile_at(t)] = jnp.transpose(qa[tile_at(t), :LANES])
        gt[:, tile_at(t)] = jnp.transpose(ga[tile_at(t), :LANES])
    for d in range(1, REACH + 1):
        forward(0, d).wait_recv()
        prepare_keys(d)
        for t in range(tiles):
            score_tile(d, t)
    for t in range(tiles):
        log_norm_tile(t)

    for d in range(REACH, -1, -1):
        dvt[...] = jnp.zeros_like(dvt)
        for t in range(tiles):
            value_tile(d, t)
        if d > 0:
            part[1, d] = dvt[...].astype(BF)
            backward(1, d).start()

    for d in range(REACH + 1):
        if d > 0:
            forward(1, d).wait_recv()
            prepare_values(d)
        for t in range(tiles):
            delta_tile(d, t)
    for t in range(tiles):
        delta_feature_tile(t)

    stores = []
    for d in range(REACH, -1, -1):
        dkt[...] = jnp.zeros_like(dkt)
        if d == 0:
            val_total = dvt[...]
            for b in range(REACH, 0, -1):
                backward(1, b).wait_recv()
                val_total = val_total + got[1, b].astype(F32)
            dv_ref[...] = jnp.transpose(val_total).astype(BF)
        for t in range(tiles):
            key_tile(d, t)
            if d == 0:
                stores.append(pltpu.make_async_copy(dq_bf.at[tile_at(t)], dq_hbm.at[tile_at(t)], store_sem.at[t]))
                stores[-1].start()
        if d > 0:
            part[0, d] = dkt[...].astype(BF)
            backward(0, d).start()

    key_total = dkt[...]
    for d in range(REACH, 0, -1):
        backward(0, d).wait_recv()
        key_total = key_total + got[0, d].astype(F32)
    dk_ref[...] = jnp.transpose(key_total).astype(BF)
    for copy in stores:
        copy.wait()
    for d in range(1, REACH + 1):
        for half in range(2):
            forward(half, d).wait_send()
            backward(half, d).wait_send()


def local(outer, inner, queries, keys, values, grad_out, doc_ids):
    tokens, heads, width = queries.shape
    rows = tokens * heads
    vmem = pltpu.VMEM
    slots = REACH + 1
    grad_queries, grad_keys, grad_values = pl.pallas_call(
        functools.partial(kernel, outer, inner),
        out_shape=(
            jax.ShapeDtypeStruct((rows, width), BF),
            jax.ShapeDtypeStruct((tokens, width), BF),
            jax.ShapeDtypeStruct((tokens, width), BF),
        ),
        in_specs=[pl.BlockSpec(memory_space=pl.ANY)] * 4 + [pl.BlockSpec(memory_space=vmem)],
        out_specs=(
            pl.BlockSpec(memory_space=pl.ANY),
            pl.BlockSpec(memory_space=vmem),
            pl.BlockSpec(memory_space=vmem),
        ),
        scratch_shapes=[
            vmem((slots, 2 * tokens + 16, width), BF),
            vmem((rows, 2 * width), BF),
            vmem((rows, 2 * width), BF),
            vmem((width, rows), BF),
            vmem((width, rows), BF),
            vmem((slots, 2 * width, tokens), BF),
            vmem((slots, 2 * width, tokens), BF),
            vmem((REACH - 1, rows, tokens), F32),
            vmem((rows, tokens + TILE), F32),
            vmem((rows, width), F32),
            vmem((rows, width), F32),
            vmem((rows, width), F32),
            vmem((width, tokens), F32),
            vmem((width, tokens), F32),
            vmem((2, slots, width, tokens), BF),
            vmem((2, slots, width, tokens), BF),
            vmem((rows, width), BF),
            pltpu.SemaphoreType.DMA((4,)),
            pltpu.SemaphoreType.DMA((tokens // TILE,)),
            pltpu.SemaphoreType.DMA((2, slots)),
            pltpu.SemaphoreType.DMA((2, slots)),
            pltpu.SemaphoreType.DMA((2, slots)),
            pltpu.SemaphoreType.DMA((2, slots)),
        ],
        compiler_params=pltpu.CompilerParams(
            collective_id=0, has_side_effects=True, vmem_limit_bytes=60 * 2**20
        ),
        cost_estimate=pl.CostEstimate(
            flops=12 * rows * 1664 * width, bytes_accessed=8 * rows * width, transcendentals=2 * rows * 1664
        ),
    )(
        queries.reshape(rows, width),
        keys,
        values,
        grad_out.reshape(rows, width),
        doc_ids.reshape(tokens // LANES, LANES),
    )
    return grad_queries.reshape(queries.shape), grad_keys, grad_values


def solution(mesh):
    both = ("outer", "inner")
    return jax.shard_map(
        functools.partial(local, mesh.shape["outer"], mesh.shape["inner"]),
        mesh=mesh,
        in_specs=(P(both, None, None), P(both, None), P(both, None), P(both, None, None), P(both)),
        out_specs=(P(both, None, None), P(both, None), P(both, None)),
        check_vma=False,
    )
```

```python
import functools
import math

import jax
import jax.numpy as jnp
from jax import lax
from jax.experimental import pallas as pl
from jax.experimental.pallas import tpu as pltpu
from jax.sharding import PartitionSpec as P

REACH = 3
MESH = pl.DeviceIdType.MESH
BIG = 1.0e30
LANES = 128
TILE = 128
SEND_ORDER = ((0, 1), (0, 2), (0, 3), (1, 1), (1, 2), (1, 3))
BF = jnp.bfloat16
F32 = jnp.float32


def nn(a, b):
    return lax.dot_general(a, b, (((1,), (0,)), ((), ())), preferred_element_type=F32)


def lane_groups(width):
    return [slice(j * LANES, (j + 1) * LANES) for j in range(width // LANES)]


def id_bits(ids, place):
    bit = lax.shift_right_logical(ids, place & 7) & 1
    return jnp.where(place < 8, bit, 1 - bit)


def three_pieces(x):
    first = x.astype(BF).astype(F32)
    second = (x - first).astype(BF).astype(F32)
    return first, second, x - first - second


def kernel(
    outer,
    inner,
    q_hbm,
    k_hbm,
    v_hbm,
    g_hbm,
    ids_ref,
    dq_hbm,
    dk_ref,
    dv_ref,
    kv,
    qa,
    ga,
    qt,
    gt,
    kat,
    vat,
    s_mid,
    s_edge,
    m_ref,
    l_ref,
    dq_acc,
    dvt,
    part,
    got,
    dq_bf,
    load_sem,
    store_sem,
    send_sem,
    recv_sem,
    back_send_sem,
    back_recv_sem,
):
    tokens = k_hbm.shape[0]
    rows = q_hbm.shape[0]
    heads = rows // tokens
    tile_rows = TILE * heads
    tiles = tokens // TILE
    scale = LANES**-0.5
    to_log2 = scale * math.log2(math.e)
    count = outer * inner
    me = lax.axis_index("outer") * inner + lax.axis_index("inner")

    def device(delta):
        there = lax.rem(me + delta + count, count)
        return (there // inner, lax.rem(there, inner))

    barrier = pltpu.get_barrier_semaphore()
    for d in range(1, REACH + 1):
        for delta in (d, -d):
            pl.semaphore_signal(barrier, inc=1, device_id=device(delta), device_id_type=MESH)

    loads = [
        pltpu.make_async_copy(k_hbm, kv.at[0, pl.ds(tokens, tokens)], load_sem.at[0]),
        pltpu.make_async_copy(v_hbm, kv.at[0, pl.ds(0, tokens)], load_sem.at[1]),
        pltpu.make_async_copy(q_hbm, qa.at[:, pl.ds(0, LANES)], load_sem.at[2]),
        pltpu.make_async_copy(g_hbm, ga.at[:, pl.ds(0, LANES)], load_sem.at[3]),
    ]
    for copy in loads:
        copy.start()
    groups = tokens // LANES
    id_rows = jnp.concatenate(
        [ids_ref[...].astype(F32), jnp.zeros((16 - groups, LANES), F32)], axis=0
    )
    kv[0, pl.ds(2 * tokens, 16)] = id_rows.astype(BF)
    loads[0].wait()
    loads[1].wait()
    pl.semaphore_wait(barrier, 2 * REACH)

    def forward(half, d):
        at = pl.ds(tokens, tokens + 16) if half == 0 else pl.ds(0, tokens)
        return pltpu.make_async_remote_copy(
            src_ref=kv.at[0, at],
            dst_ref=kv.at[d, at],
            send_sem=send_sem.at[half, d],
            recv_sem=recv_sem.at[half, d],
            device_id=device(d),
            device_id_type=MESH,
        )

    def backward(half, d):
        return pltpu.make_async_remote_copy(
            src_ref=part.at[half, d],
            dst_ref=got.at[half, d],
            send_sem=back_send_sem.at[half, d],
            recv_sem=back_recv_sem.at[half, d],
            device_id=device(-d),
            device_id_type=MESH,
        )

    for half, d in SEND_ORDER:
        forward(half, d).start()

    lane = lax.broadcasted_iota(jnp.int32, (LANES, LANES), 1)
    sub = lax.broadcasted_iota(jnp.int32, (LANES, LANES), 0)
    own_ids = ids_ref[...].astype(F32)
    for t in range(groups):
        ids_t = jnp.transpose(jnp.broadcast_to(own_ids[t : t + 1], (LANES, LANES)))
        feature = jnp.where(lane < 16, id_bits(ids_t.astype(jnp.int32), lane), 0).astype(F32)
        spread = jnp.broadcast_to(feature[:, None, :], (LANES, heads, LANES))
        at = pl.ds(t * LANES * heads, LANES * heads)
        qa[at, LANES:] = spread.reshape(LANES * heads, LANES).astype(BF)

    def prepare_keys(d):
        kat[d, :LANES] = jnp.transpose(kv[d, pl.ds(tokens, tokens)])
        ids = kv[d, pl.ds(2 * tokens, 16)].astype(F32)
        for j in range(groups):
            ids_j = jnp.broadcast_to(ids[j : j + 1], (LANES, LANES)).astype(jnp.int32)
            unequal = jnp.where((id_bits(ids_j, sub) == 0) & (sub < 16), -BIG, 0.0)
            kat[d, LANES:, j * LANES : (j + 1) * LANES] = unequal.astype(BF)

    def prepare_values(d):
        vat[d, :LANES] = jnp.transpose(kv[d, pl.ds(0, tokens)])
        ones = jnp.where(lax.broadcasted_iota(jnp.int32, (LANES, tokens), 0) < 3, 1.0, 0.0)
        vat[d, LANES:] = ones.astype(BF)

    tile_token = lax.broadcasted_iota(jnp.int32, (tile_rows, LANES), 0) // heads
    tile_key = lax.broadcasted_iota(jnp.int32, (tile_rows, LANES), 1)

    def tile_at(t):
        return pl.ds(t * tile_rows, tile_rows)

    def keys_of(d, t):
        if d == 0:
            return 0, (t + 1) * TILE
        if d == REACH:
            return t * TILE, tokens - t * TILE
        return 0, tokens

    def stored(d, t):
        if d == 0:
            return s_edge.at[tile_at(t), pl.ds(0, (t + 1) * TILE)]
        if d == REACH:
            return s_edge.at[tile_at(t), pl.ds((t + 1) * TILE, tokens - t * TILE)]
        return s_mid.at[d - 1, tile_at(t)]

    def score_tile(d, t):
        rows_at = tile_at(t)
        start, width = keys_of(d, t)
        scores = nn(qa[rows_at, :], kat[d, :, pl.ds(start, width)])
        pieces = [scores[:, g] for g in lane_groups(width)]
        if d == 0:
            for j in range(TILE // LANES):
                k = j - TILE // LANES
                pieces[k] = jnp.where(tile_key + j * LANES <= tile_token, pieces[k], -BIG)
        top = functools.reduce(jnp.maximum, pieces)
        norm = None
        if d > 0:
            before = m_ref[rows_at, :]
            top = jnp.maximum(top, before)
            norm = l_ref[rows_at, :] * jnp.exp2((before - top) * to_log2)
        m_ref[rows_at, :] = top
        place = stored(d, t)
        for piece, g in zip(pieces, lane_groups(width)):
            place[:, g] = piece
            e = jnp.exp2((piece - top) * to_log2)
            norm = e if norm is None else norm + e
        l_ref[rows_at, :] = norm

    def log_norm_tile(t):
        rows_at = tile_at(t)
        m = m_ref[rows_at, :]
        top = jnp.max(m, axis=1, keepdims=True)
        norm = jnp.sum(l_ref[rows_at, :] * jnp.exp2((m - top) * to_log2), axis=1, keepdims=True)
        m_ref[rows_at, :] = jnp.broadcast_to(top * to_log2 + jnp.log2(norm), (tile_rows, LANES))

    def value_tile(d, t):
        rows_at = tile_at(t)
        start, width = keys_of(d, t)
        dprob = nn(ga[rows_at, :LANES], vat[d, :LANES, pl.ds(start, width)])
        log_norm = m_ref[rows_at, :]
        place = stored(d, t)
        total = None if d == 0 else l_ref[rows_at, :]
        probs = []
        for g in lane_groups(width):
            p = jnp.exp2(place[:, g] * to_log2 - log_norm)
            place[:, g] = p
            probs.append(p.astype(BF))
            pd = p * dprob[:, g]
            total = pd if total is None else total + pd
        l_ref[rows_at, :] = total
        probs = jnp.concatenate(probs, axis=1) if len(probs) > 1 else probs[0]
        return nn(gt[:, rows_at], probs)

    def delta_feature_tile(t):
        rows_at = tile_at(t)
        pieces = three_pieces(-jnp.sum(l_ref[rows_at, :], axis=1, keepdims=True))
        feature = jnp.zeros((tile_rows, LANES), F32)
        for j, piece in enumerate(pieces):
            feature = jnp.where(tile_key == j, piece, feature)
        ga[rows_at, LANES:] = feature.astype(BF)

    def key_tile(d, t):
        rows_at = tile_at(t)
        start, width = keys_of(d, t)
        centred = nn(ga[rows_at, :], vat[d, :, pl.ds(start, width)])
        place = stored(d, t)
        dscores = [(place[:, g] * centred[:, g] * scale).astype(BF) for g in lane_groups(width)]
        dscores = jnp.concatenate(dscores, axis=1) if len(dscores) > 1 else dscores[0]
        key_sum = nn(qt[:, rows_at], dscores)
        dq = nn(dscores, kv[d, pl.ds(tokens + start, width), :])
        if d == REACH:
            dq_acc[rows_at, :] = dq
        elif d > 0:
            dq_acc[rows_at, :] += dq
        else:
            dq_bf[rows_at, :] = (dq_acc[rows_at, :] + dq).astype(BF)
        return key_sum

    def add_up(sums, d, t, term):
        start, width = keys_of(d, t)
        for j, g in enumerate(lane_groups(width)):
            at = start // LANES + j
            sums[at] = term[:, g] if sums[at] is None else sums[at] + term[:, g]

    loads[2].wait()
    loads[3].wait()
    prepare_keys(0)
    prepare_values(0)
    for t in range(tiles):
        score_tile(0, t)
    for t in range(tiles):
        qt[:, tile_at(t)] = jnp.transpose(qa[tile_at(t), :LANES])
        gt[:, tile_at(t)] = jnp.transpose(ga[tile_at(t), :LANES])
    for d in range(1, REACH + 1):
        forward(0, d).wait_recv()
        prepare_keys(d)
        for t in range(tiles):
            score_tile(d, t)
    for t in range(tiles):
        log_norm_tile(t)

    for d in range(REACH + 1):
        if d > 0:
            forward(1, d).wait_recv()
            prepare_values(d)
        sums = [None] * groups
        for t in range(tiles):
            add_up(sums, d, t, value_tile(d, t))
        for j, g in enumerate(lane_groups(tokens)):
            if d > 0:
                part[1, d, :, g] = sums[j].astype(BF)
            else:
                dvt[:, g] = sums[j]
        if d > 0:
            backward(1, d).start()

    for t in range(tiles):
        delta_feature_tile(t)

    stores = []
    for d in range(REACH, -1, -1):
        sums = [None] * groups
        if d == 0:
            val_total = dvt[...]
            for b in range(REACH, 0, -1):
                backward(1, b).wait_recv()
                val_total = val_total + got[1, b].astype(F32)
            dv_ref[...] = jnp.transpose(val_total).astype(BF)
        for t in range(tiles):
            add_up(sums, d, t, key_tile(d, t))
            if d == 0:
                stores.append(pltpu.make_async_copy(dq_bf.at[tile_at(t)], dq_hbm.at[tile_at(t)], store_sem.at[t]))
                stores[-1].start()
        if d > 0:
            for j, g in enumerate(lane_groups(tokens)):
                part[0, d, :, g] = sums[j].astype(BF)
            backward(0, d).start()

    key_total = jnp.concatenate(sums, axis=1)
    for d in range(REACH, 0, -1):
        backward(0, d).wait_recv()
        key_total = key_total + got[0, d].astype(F32)
    dk_ref[...] = jnp.transpose(key_total).astype(BF)
    for copy in stores:
        copy.wait()
    for d in range(1, REACH + 1):
        for half in range(2):
            forward(half, d).wait_send()
            backward(half, d).wait_send()


def finish(dq_in, dk_in, dv_in, dq_out, dk_out, dv_out):
    for taken, given in ((dq_in, dq_out), (dk_in, dk_out), (dv_in, dv_out)):
        given[...] = taken[...]


def local(outer, inner, queries, keys, values, grad_out, doc_ids):
    tokens, heads, width = queries.shape
    rows = tokens * heads
    vmem = pltpu.VMEM
    slots = REACH + 1
    grad_queries, grad_keys, grad_values = pl.pallas_call(
        functools.partial(kernel, outer, inner),
        out_shape=(
            jax.ShapeDtypeStruct((rows, width), BF),
            jax.ShapeDtypeStruct((tokens, width), BF),
            jax.ShapeDtypeStruct((tokens, width), BF),
        ),
        in_specs=[pl.BlockSpec(memory_space=pl.ANY)] * 4 + [pl.BlockSpec(memory_space=vmem)],
        out_specs=(
            pl.BlockSpec(memory_space=pl.ANY),
            pl.BlockSpec(memory_space=vmem),
            pl.BlockSpec(memory_space=vmem),
        ),
        scratch_shapes=[
            vmem((slots, 2 * tokens + 16, width), BF),
            vmem((rows, 2 * width), BF),
            vmem((rows, 2 * width), BF),
            vmem((width, rows), BF),
            vmem((width, rows), BF),
            vmem((slots, 2 * width, tokens), BF),
            vmem((slots, 2 * width, tokens), BF),
            vmem((REACH - 1, rows, tokens), F32),
            vmem((rows, tokens + TILE), F32),
            vmem((rows, width), F32),
            vmem((rows, width), F32),
            vmem((rows, width), F32),
            vmem((width, tokens), F32),
            vmem((2, slots, width, tokens), BF),
            vmem((2, slots, width, tokens), BF),
            vmem((rows, width), BF),
            pltpu.SemaphoreType.DMA((4,)),
            pltpu.SemaphoreType.DMA((tokens // TILE,)),
            pltpu.SemaphoreType.DMA((2, slots)),
            pltpu.SemaphoreType.DMA((2, slots)),
            pltpu.SemaphoreType.DMA((2, slots)),
            pltpu.SemaphoreType.DMA((2, slots)),
        ],
        compiler_params=pltpu.CompilerParams(
            collective_id=0, has_side_effects=True, vmem_limit_bytes=60 * 2**20
        ),
        cost_estimate=pl.CostEstimate(
            flops=12 * rows * 1664 * width, bytes_accessed=8 * rows * width, transcendentals=2 * rows * 1664
        ),
    )(
        queries.reshape(rows, width),
        keys,
        values,
        grad_out.reshape(rows, width),
        doc_ids.reshape(tokens // LANES, LANES),
    )
    grad_queries, grad_keys, grad_values = pl.pallas_call(
        finish,
        out_shape=(
            jax.ShapeDtypeStruct((rows, width), BF),
            jax.ShapeDtypeStruct((tokens, width), BF),
            jax.ShapeDtypeStruct((tokens, width), BF),
        ),
        in_specs=[pl.BlockSpec(memory_space=vmem)] * 3,
        out_specs=[pl.BlockSpec(memory_space=vmem)] * 3,
    )(grad_queries, grad_keys, grad_values)
    return grad_queries.reshape(queries.shape), grad_keys, grad_values


def solution(mesh):
    both = ("outer", "inner")
    return jax.shard_map(
        functools.partial(local, mesh.shape["outer"], mesh.shape["inner"]),
        mesh=mesh,
        in_specs=(P(both, None, None), P(both, None), P(both, None), P(both, None, None), P(both)),
        out_specs=(P(both, None, None), P(both, None), P(both, None)),
        check_vma=False,
    )
```

```python
import functools
import math

import jax
import jax.numpy as jnp
from jax import lax
from jax.experimental import pallas as pl
from jax.experimental.pallas import tpu as pltpu
from jax.sharding import PartitionSpec as P

REACH = 3
MESH = pl.DeviceIdType.MESH
BIG = 1.0e30
LANES = 128
TILE = 128
SEND_ORDER = ((2, 1), (2, 2), (2, 3), (0, 1), (0, 2), (0, 3), (1, 1), (1, 2), (1, 3))
BF = jnp.bfloat16
F32 = jnp.float32


def nn(a, b):
    return lax.dot_general(a, b, (((1,), (0,)), ((), ())), preferred_element_type=F32)


def lane_groups(width):
    return [slice(j * LANES, (j + 1) * LANES) for j in range(width // LANES)]


def id_bits(ids, place):
    bit = lax.shift_right_logical(ids, place & 7) & 1
    return jnp.where(place < 8, bit, 1 - bit)


def three_pieces(x):
    first = x.astype(BF).astype(F32)
    second = (x - first).astype(BF).astype(F32)
    return first, second, x - first - second


def kernel(
    outer,
    inner,
    q_hbm,
    k_hbm,
    v_hbm,
    g_hbm,
    ids_ref,
    dq_hbm,
    dk_ref,
    dv_ref,
    kv,
    qa,
    ga,
    qt,
    gt,
    kat,
    vat,
    s_mid,
    s_edge,
    m_ref,
    l_ref,
    dq_acc,
    dvt,
    part,
    got,
    dq_bf,
    load_sem,
    store_sem,
    send_sem,
    recv_sem,
    back_send_sem,
    back_recv_sem,
):
    tokens = k_hbm.shape[0]
    rows = q_hbm.shape[0]
    heads = rows // tokens
    tile_rows = TILE * heads
    tiles = tokens // TILE
    scale = LANES**-0.5
    to_log2 = scale * math.log2(math.e)
    count = outer * inner
    me = lax.axis_index("outer") * inner + lax.axis_index("inner")

    def device(delta):
        there = lax.rem(me + delta + count, count)
        return (there // inner, lax.rem(there, inner))

    barrier = pltpu.get_barrier_semaphore()
    for d in range(1, REACH + 1):
        for delta in (d, -d):
            pl.semaphore_signal(barrier, inc=1, device_id=device(delta), device_id_type=MESH)

    loads = [
        pltpu.make_async_copy(k_hbm, kv.at[0, pl.ds(tokens, tokens)], load_sem.at[0]),
        pltpu.make_async_copy(v_hbm, kv.at[0, pl.ds(0, tokens)], load_sem.at[1]),
        pltpu.make_async_copy(q_hbm, qa.at[:, pl.ds(0, LANES)], load_sem.at[2]),
        pltpu.make_async_copy(g_hbm, ga.at[:, pl.ds(0, LANES)], load_sem.at[3]),
    ]
    for copy in loads:
        copy.start()
    groups = tokens // LANES
    id_rows = jnp.concatenate(
        [ids_ref[...].astype(F32), jnp.zeros((16 - groups, LANES), F32)], axis=0
    )
    kv[0, pl.ds(2 * tokens, 16)] = id_rows.astype(BF)
    pl.semaphore_wait(barrier, 2 * REACH)

    def forward(half, d):
        at = (pl.ds(tokens, tokens), pl.ds(0, tokens), pl.ds(2 * tokens, 16))[half]
        return pltpu.make_async_remote_copy(
            src_ref=k_hbm if half == 0 else kv.at[0, at],
            dst_ref=kv.at[d, at],
            send_sem=send_sem.at[half, d],
            recv_sem=recv_sem.at[half, d],
            device_id=device(d),
            device_id_type=MESH,
        )

    def backward(half, d):
        return pltpu.make_async_remote_copy(
            src_ref=part.at[half, d],
            dst_ref=got.at[half, d],
            send_sem=back_send_sem.at[half, d],
            recv_sem=back_recv_sem.at[half, d],
            device_id=device(-d),
            device_id_type=MESH,
        )

    for half, d in SEND_ORDER:
        if (half, d) == (1, 1):
            loads[1].wait()
        forward(half, d).start()

    lane = lax.broadcasted_iota(jnp.int32, (LANES, LANES), 1)
    sub = lax.broadcasted_iota(jnp.int32, (LANES, LANES), 0)
    own_ids = ids_ref[...].astype(F32)
    for t in range(groups):
        ids_t = jnp.transpose(jnp.broadcast_to(own_ids[t : t + 1], (LANES, LANES)))
        feature = jnp.where(lane < 16, id_bits(ids_t.astype(jnp.int32), lane), 0).astype(F32)
        spread = jnp.broadcast_to(feature[:, None, :], (LANES, heads, LANES))
        at = pl.ds(t * LANES * heads, LANES * heads)
        qa[at, LANES:] = spread.reshape(LANES * heads, LANES).astype(BF)

    def prepare_keys(d):
        kat[d, :LANES] = jnp.transpose(kv[d, pl.ds(tokens, tokens)])
        ids = kv[d, pl.ds(2 * tokens, 16)].astype(F32)
        for j in range(groups):
            ids_j = jnp.broadcast_to(ids[j : j + 1], (LANES, LANES)).astype(jnp.int32)
            unequal = jnp.where((id_bits(ids_j, sub) == 0) & (sub < 16), -BIG, 0.0)
            kat[d, LANES:, j * LANES : (j + 1) * LANES] = unequal.astype(BF)

    def prepare_values(d):
        vat[d, :LANES] = jnp.transpose(kv[d, pl.ds(0, tokens)])
        ones = jnp.where(lax.broadcasted_iota(jnp.int32, (LANES, tokens), 0) < 3, 1.0, 0.0)
        vat[d, LANES:] = ones.astype(BF)

    tile_token = lax.broadcasted_iota(jnp.int32, (tile_rows, LANES), 0) // heads
    tile_key = lax.broadcasted_iota(jnp.int32, (tile_rows, LANES), 1)

    def tile_at(t):
        return pl.ds(t * tile_rows, tile_rows)

    def keys_of(d, t):
        if d == 0:
            return 0, (t + 1) * TILE
        if d == REACH:
            return t * TILE, tokens - t * TILE
        return 0, tokens

    def stored(d, t):
        if d == 0:
            return s_edge.at[tile_at(t), pl.ds(0, (t + 1) * TILE)]
        if d == REACH:
            return s_edge.at[tile_at(t), pl.ds((t + 1) * TILE, tokens - t * TILE)]
        return s_mid.at[d - 1, tile_at(t)]

    def score_tile(d, t):
        rows_at = tile_at(t)
        start, width = keys_of(d, t)
        scores = nn(qa[rows_at, :], kat[d, :, pl.ds(start, width)])
        pieces = [scores[:, g] for g in lane_groups(width)]
        if d == 0:
            for j in range(TILE // LANES):
                k = j - TILE // LANES
                pieces[k] = jnp.where(tile_key + j * LANES <= tile_token, pieces[k], -BIG)
        top = functools.reduce(jnp.maximum, pieces)
        norm = None
        if d > 0:
            before = m_ref[rows_at, :]
            top = jnp.maximum(top, before)
            norm = l_ref[rows_at, :] * jnp.exp2((before - top) * to_log2)
        m_ref[rows_at, :] = top
        place = stored(d, t)
        for piece, g in zip(pieces, lane_groups(width)):
            place[:, g] = piece
            e = jnp.exp2((piece - top) * to_log2)
            norm = e if norm is None else norm + e
        l_ref[rows_at, :] = norm

    def log_norm_tile(t):
        rows_at = tile_at(t)
        m = m_ref[rows_at, :]
        top = jnp.max(m, axis=1, keepdims=True)
        norm = jnp.sum(l_ref[rows_at, :] * jnp.exp2((m - top) * to_log2), axis=1, keepdims=True)
        m_ref[rows_at, :] = jnp.broadcast_to(top * to_log2 + jnp.log2(norm), (tile_rows, LANES))

    def value_tile(d, t):
        rows_at = tile_at(t)
        start, width = keys_of(d, t)
        dprob = nn(ga[rows_at, :LANES], vat[d, :LANES, pl.ds(start, width)])
        log_norm = m_ref[rows_at, :]
        place = stored(d, t)
        total = None if d == 0 else l_ref[rows_at, :]
        probs = []
        for g in lane_groups(width):
            p = jnp.exp2(place[:, g] * to_log2 - log_norm)
            place[:, g] = p
            probs.append(p.astype(BF))
            pd = p * dprob[:, g]
            total = pd if total is None else total + pd
        l_ref[rows_at, :] = total
        probs = jnp.concatenate(probs, axis=1) if len(probs) > 1 else probs[0]
        return nn(gt[:, rows_at], probs)

    def delta_feature_tile(t):
        rows_at = tile_at(t)
        pieces = three_pieces(-jnp.sum(l_ref[rows_at, :], axis=1, keepdims=True))
        feature = jnp.zeros((tile_rows, LANES), F32)
        for j, piece in enumerate(pieces):
            feature = jnp.where(tile_key == j, piece, feature)
        ga[rows_at, LANES:] = feature.astype(BF)

    def key_tile(d, t):
        rows_at = tile_at(t)
        start, width = keys_of(d, t)
        centred = nn(ga[rows_at, :], vat[d, :, pl.ds(start, width)])
        place = stored(d, t)
        dscores = [(place[:, g] * centred[:, g] * scale).astype(BF) for g in lane_groups(width)]
        dscores = jnp.concatenate(dscores, axis=1) if len(dscores) > 1 else dscores[0]
        key_sum = nn(qt[:, rows_at], dscores)
        dq = nn(dscores, kv[d, pl.ds(tokens + start, width), :])
        if d == REACH:
            dq_acc[rows_at, :] = dq
        elif d > 0:
            dq_acc[rows_at, :] += dq
        else:
            dq_bf[rows_at, :] = (dq_acc[rows_at, :] + dq).astype(BF)
        return key_sum

    def add_up(sums, d, t, term):
        start, width = keys_of(d, t)
        for j, g in enumerate(lane_groups(width)):
            at = start // LANES + j
            sums[at] = term[:, g] if sums[at] is None else sums[at] + term[:, g]

    for copy in (loads[0], loads[2], loads[3]):
        copy.wait()
    prepare_keys(0)
    prepare_values(0)
    for t in range(tiles):
        score_tile(0, t)
    for t in range(tiles):
        qt[:, tile_at(t)] = jnp.transpose(qa[tile_at(t), :LANES])
        gt[:, tile_at(t)] = jnp.transpose(ga[tile_at(t), :LANES])
    for d in range(1, REACH + 1):
        forward(2, d).wait_recv()
        forward(0, d).wait_recv()
        prepare_keys(d)
        for t in range(tiles):
            score_tile(d, t)
    for t in range(tiles):
        log_norm_tile(t)

    for d in range(REACH + 1):
        if d > 0:
            forward(1, d).wait_recv()
            prepare_values(d)
        sums = [None] * groups
        for t in range(tiles):
            add_up(sums, d, t, value_tile(d, t))
        for j, g in enumerate(lane_groups(tokens)):
            if d > 0:
                part[1, d, :, g] = sums[j].astype(BF)
            else:
                dvt[:, g] = sums[j]
        if d > 0:
            backward(1, d).start()

    for t in range(tiles):
        delta_feature_tile(t)

    stores = []
    for d in range(REACH, -1, -1):
        sums = [None] * groups
        if d == 0:
            val_total = dvt[...]
            for b in range(REACH, 0, -1):
                backward(1, b).wait_recv()
                val_total = val_total + got[1, b].astype(F32)
            dv_ref[...] = jnp.transpose(val_total).astype(BF)
        for t in range(tiles):
            add_up(sums, d, t, key_tile(d, t))
            if d == 0:
                stores.append(pltpu.make_async_copy(dq_bf.at[tile_at(t)], dq_hbm.at[tile_at(t)], store_sem.at[t]))
                stores[-1].start()
        if d > 0:
            for j, g in enumerate(lane_groups(tokens)):
                part[0, d, :, g] = sums[j].astype(BF)
            backward(0, d).start()

    key_total = jnp.concatenate(sums, axis=1)
    for d in range(REACH, 0, -1):
        backward(0, d).wait_recv()
        key_total = key_total + got[0, d].astype(F32)
    dk_ref[...] = jnp.transpose(key_total).astype(BF)
    for copy in stores:
        copy.wait()
    for d in range(1, REACH + 1):
        for half in range(2):
            forward(half, d).wait_send()
            backward(half, d).wait_send()
        forward(2, d).wait_send()


def finish(dq_in, dk_in, dv_in, dq_out, dk_out, dv_out):
    for taken, given in ((dq_in, dq_out), (dk_in, dk_out), (dv_in, dv_out)):
        given[...] = taken[...]


def local(outer, inner, queries, keys, values, grad_out, doc_ids):
    tokens, heads, width = queries.shape
    rows = tokens * heads
    vmem = pltpu.VMEM
    slots = REACH + 1
    grad_queries, grad_keys, grad_values = pl.pallas_call(
        functools.partial(kernel, outer, inner),
        out_shape=(
            jax.ShapeDtypeStruct((rows, width), BF),
            jax.ShapeDtypeStruct((tokens, width), BF),
            jax.ShapeDtypeStruct((tokens, width), BF),
        ),
        in_specs=[pl.BlockSpec(memory_space=pl.ANY)] * 4 + [pl.BlockSpec(memory_space=vmem)],
        out_specs=(
            pl.BlockSpec(memory_space=pl.ANY),
            pl.BlockSpec(memory_space=vmem),
            pl.BlockSpec(memory_space=vmem),
        ),
        scratch_shapes=[
            vmem((slots, 2 * tokens + 16, width), BF),
            vmem((rows, 2 * width), BF),
            vmem((rows, 2 * width), BF),
            vmem((width, rows), BF),
            vmem((width, rows), BF),
            vmem((slots, 2 * width, tokens), BF),
            vmem((slots, 2 * width, tokens), BF),
            vmem((REACH - 1, rows, tokens), F32),
            vmem((rows, tokens + TILE), F32),
            vmem((rows, width), F32),
            vmem((rows, width), F32),
            vmem((rows, width), F32),
            vmem((width, tokens), F32),
            vmem((2, slots, width, tokens), BF),
            vmem((2, slots, width, tokens), BF),
            vmem((rows, width), BF),
            pltpu.SemaphoreType.DMA((4,)),
            pltpu.SemaphoreType.DMA((tokens // TILE,)),
            pltpu.SemaphoreType.DMA((3, slots)),
            pltpu.SemaphoreType.DMA((3, slots)),
            pltpu.SemaphoreType.DMA((2, slots)),
            pltpu.SemaphoreType.DMA((2, slots)),
        ],
        compiler_params=pltpu.CompilerParams(
            collective_id=0, has_side_effects=True, vmem_limit_bytes=60 * 2**20
        ),
        cost_estimate=pl.CostEstimate(
            flops=12 * rows * 1664 * width, bytes_accessed=8 * rows * width, transcendentals=2 * rows * 1664
        ),
    )(
        queries.reshape(rows, width),
        keys,
        values,
        grad_out.reshape(rows, width),
        doc_ids.reshape(tokens // LANES, LANES),
    )
    grad_queries, grad_keys, grad_values = pl.pallas_call(
        finish,
        out_shape=(
            jax.ShapeDtypeStruct((rows, width), BF),
            jax.ShapeDtypeStruct((tokens, width), BF),
            jax.ShapeDtypeStruct((tokens, width), BF),
        ),
        in_specs=[pl.BlockSpec(memory_space=vmem)] * 3,
        out_specs=[pl.BlockSpec(memory_space=vmem)] * 3,
    )(grad_queries, grad_keys, grad_values)
    return grad_queries.reshape(queries.shape), grad_keys, grad_values


def solution(mesh):
    both = ("outer", "inner")
    return jax.shard_map(
        functools.partial(local, mesh.shape["outer"], mesh.shape["inner"]),
        mesh=mesh,
        in_specs=(P(both, None, None), P(both, None), P(both, None), P(both, None, None), P(both)),
        out_specs=(P(both, None, None), P(both, None), P(both, None)),
        check_vma=False,
    )
```

```python
import functools
import math

import jax
import jax.numpy as jnp
from jax import lax
from jax.experimental import pallas as pl
from jax.experimental.pallas import tpu as pltpu
from jax.sharding import PartitionSpec as P

REACH = 3
MESH = pl.DeviceIdType.MESH
BIG = 1.0e30
LANES = 128
TILE = 128
SEND_ORDER = ((2, 1), (2, 2), (2, 3), (0, 1), (0, 2), (0, 3), (1, 1), (1, 2), (1, 3))
BF = jnp.bfloat16
F32 = jnp.float32


def nn(a, b):
    return lax.dot_general(a, b, (((1,), (0,)), ((), ())), preferred_element_type=F32)


def lane_groups(width):
    return [slice(j * LANES, (j + 1) * LANES) for j in range(width // LANES)]


def id_bits(ids, place):
    bit = lax.shift_right_logical(ids, place & 7) & 1
    return jnp.where(place < 8, bit, 1 - bit)


def three_pieces(x):
    first = x.astype(BF).astype(F32)
    second = (x - first).astype(BF).astype(F32)
    return first, second, x - first - second


def kernel(
    outer,
    inner,
    q_hbm,
    k_hbm,
    v_hbm,
    g_hbm,
    ids_ref,
    dq_hbm,
    dk_ref,
    dv_ref,
    kv,
    qa,
    ga,
    qt,
    gt,
    kat,
    vat,
    s_mid,
    s_edge,
    m_ref,
    l_ref,
    dq_acc,
    dvt,
    part,
    got,
    dq_bf,
    load_sem,
    store_sem,
    send_sem,
    recv_sem,
    back_send_sem,
    back_recv_sem,
):
    tokens = k_hbm.shape[0]
    rows = q_hbm.shape[0]
    heads = rows // tokens
    tile_rows = TILE * heads
    tiles = tokens // TILE
    scale = LANES**-0.5
    to_log2 = scale * math.log2(math.e)
    count = outer * inner
    me = lax.axis_index("outer") * inner + lax.axis_index("inner")

    def device(delta):
        there = lax.rem(me + delta + count, count)
        return (there // inner, lax.rem(there, inner))

    barrier = pltpu.get_barrier_semaphore()
    for d in range(1, REACH + 1):
        for delta in (d, -d):
            pl.semaphore_signal(barrier, inc=1, device_id=device(delta), device_id_type=MESH)

    loads = [
        pltpu.make_async_copy(k_hbm, kv.at[0, pl.ds(tokens, tokens)], load_sem.at[0]),
        pltpu.make_async_copy(v_hbm, kv.at[0, pl.ds(0, tokens)], load_sem.at[1]),
        pltpu.make_async_copy(q_hbm, qa.at[:, pl.ds(0, LANES)], load_sem.at[2]),
        pltpu.make_async_copy(g_hbm, ga.at[:, pl.ds(0, LANES)], load_sem.at[3]),
    ]
    for copy in loads:
        copy.start()
    groups = tokens // LANES
    id_rows = jnp.concatenate(
        [ids_ref[...].astype(F32), jnp.zeros((16 - groups, LANES), F32)], axis=0
    )
    kv[0, pl.ds(2 * tokens, 16)] = id_rows.astype(BF)
    pl.semaphore_wait(barrier, 2 * REACH)

    def forward(half, d):
        at = (pl.ds(tokens, tokens), pl.ds(0, tokens), pl.ds(2 * tokens, 16))[half]
        return pltpu.make_async_remote_copy(
            src_ref=k_hbm if half == 0 else kv.at[0, at],
            dst_ref=kv.at[d, at],
            send_sem=send_sem.at[half, d],
            recv_sem=recv_sem.at[half, d],
            device_id=device(d),
            device_id_type=MESH,
        )

    def backward(half, d):
        return pltpu.make_async_remote_copy(
            src_ref=part.at[half, d],
            dst_ref=got.at[half, d],
            send_sem=back_send_sem.at[half, d],
            recv_sem=back_recv_sem.at[half, d],
            device_id=device(-d),
            device_id_type=MESH,
        )

    for half, d in SEND_ORDER:
        if (half, d) == (1, 1):
            loads[1].wait()
        forward(half, d).start()

    lane = lax.broadcasted_iota(jnp.int32, (LANES, LANES), 1)
    sub = lax.broadcasted_iota(jnp.int32, (LANES, LANES), 0)
    own_ids = ids_ref[...].astype(F32)
    for t in range(groups):
        ids_t = jnp.transpose(jnp.broadcast_to(own_ids[t : t + 1], (LANES, LANES)))
        feature = jnp.where(lane < 16, id_bits(ids_t.astype(jnp.int32), lane), 0).astype(F32)
        spread = jnp.broadcast_to(feature[:, None, :], (LANES, heads, LANES))
        at = pl.ds(t * LANES * heads, LANES * heads)
        qa[at, LANES:] = spread.reshape(LANES * heads, LANES).astype(BF)

    def prepare_keys(d):
        kat[d, :LANES] = jnp.transpose(kv[d, pl.ds(tokens, tokens)])
        ids = kv[d, pl.ds(2 * tokens, 16)].astype(F32)
        for j in range(groups):
            ids_j = jnp.broadcast_to(ids[j : j + 1], (LANES, LANES)).astype(jnp.int32)
            unequal = jnp.where((id_bits(ids_j, sub) == 0) & (sub < 16), -BIG, 0.0)
            kat[d, LANES:, j * LANES : (j + 1) * LANES] = unequal.astype(BF)

    def prepare_values(d):
        vat[d, :LANES] = jnp.transpose(kv[d, pl.ds(0, tokens)])
        ones = jnp.where(lax.broadcasted_iota(jnp.int32, (LANES, tokens), 0) < 3, 1.0, 0.0)
        vat[d, LANES:] = ones.astype(BF)

    tile_token = lax.broadcasted_iota(jnp.int32, (tile_rows, LANES), 0) // heads
    tile_key = lax.broadcasted_iota(jnp.int32, (tile_rows, LANES), 1)

    def tile_at(t):
        return pl.ds(t * tile_rows, tile_rows)

    def keys_of(d, t):
        if d == 0:
            return 0, (t + 1) * TILE
        if d == REACH:
            return t * TILE, tokens - t * TILE
        return 0, tokens

    def stored(d, t):
        if d == 0:
            return s_edge.at[tile_at(t), pl.ds(0, (t + 1) * TILE)]
        if d == REACH:
            return s_edge.at[tile_at(t), pl.ds((t + 1) * TILE, tokens - t * TILE)]
        return s_mid.at[d - 1, tile_at(t)]

    def score_tile(d, t):
        rows_at = tile_at(t)
        start, width = keys_of(d, t)
        scores = nn(qa[rows_at, :], kat[d, :, pl.ds(start, width)])
        pieces = [scores[:, g] for g in lane_groups(width)]
        if d == 0:
            for j in range(TILE // LANES):
                k = j - TILE // LANES
                pieces[k] = jnp.where(tile_key + j * LANES <= tile_token, pieces[k], -BIG)
        top = functools.reduce(jnp.maximum, pieces)
        norm = None
        if d > 0:
            before = m_ref[rows_at, :]
            top = jnp.maximum(top, before)
            norm = l_ref[rows_at, :] * jnp.exp2((before - top) * to_log2)
        m_ref[rows_at, :] = top
        place = stored(d, t)
        for piece, g in zip(pieces, lane_groups(width)):
            place[:, g] = piece
            e = jnp.exp2((piece - top) * to_log2)
            norm = e if norm is None else norm + e
        l_ref[rows_at, :] = norm

    def log_norm_tile(t):
        rows_at = tile_at(t)
        m = m_ref[rows_at, :]
        top = jnp.max(m, axis=1, keepdims=True)
        norm = jnp.sum(l_ref[rows_at, :] * jnp.exp2((m - top) * to_log2), axis=1, keepdims=True)
        m_ref[rows_at, :] = jnp.broadcast_to(top * to_log2 + jnp.log2(norm), (tile_rows, LANES))

    def value_tile(d, t):
        rows_at = tile_at(t)
        start, width = keys_of(d, t)
        dprob = nn(ga[rows_at, :LANES], vat[d, :LANES, pl.ds(start, width)])
        log_norm = m_ref[rows_at, :]
        place = stored(d, t)
        total = None if d == 0 else l_ref[rows_at, :]
        probs = []
        for g in lane_groups(width):
            p = jnp.exp2(place[:, g] * to_log2 - log_norm)
            place[:, g] = p
            probs.append(p.astype(BF))
            pd = p * dprob[:, g]
            total = pd if total is None else total + pd
        l_ref[rows_at, :] = total
        probs = jnp.concatenate(probs, axis=1) if len(probs) > 1 else probs[0]
        return nn(gt[:, rows_at], probs)

    def delta_feature_tile(t):
        rows_at = tile_at(t)
        pieces = three_pieces(-jnp.sum(l_ref[rows_at, :], axis=1, keepdims=True))
        feature = jnp.zeros((tile_rows, LANES), F32)
        for j, piece in enumerate(pieces):
            feature = jnp.where(tile_key == j, piece, feature)
        ga[rows_at, LANES:] = feature.astype(BF)

    def key_tile(d, t):
        rows_at = tile_at(t)
        start, width = keys_of(d, t)
        centred = nn(ga[rows_at, :], vat[d, :, pl.ds(start, width)])
        place = stored(d, t)
        dscores = [(place[:, g] * centred[:, g] * scale).astype(BF) for g in lane_groups(width)]
        dscores = jnp.concatenate(dscores, axis=1) if len(dscores) > 1 else dscores[0]
        key_sum = nn(qt[:, rows_at], dscores)
        dq = nn(dscores, kv[d, pl.ds(tokens + start, width), :])
        if d == REACH:
            dq_acc[rows_at, :] = dq
        elif d > 0:
            dq_acc[rows_at, :] += dq
        else:
            dq_bf[rows_at, :] = (dq_acc[rows_at, :] + dq).astype(BF)
        return key_sum

    def add_up(sums, d, t, term):
        start, width = keys_of(d, t)
        for j, g in enumerate(lane_groups(width)):
            at = start // LANES + j
            sums[at] = term[:, g] if sums[at] is None else sums[at] + term[:, g]

    for copy in (loads[0], loads[2], loads[3]):
        copy.wait()
    prepare_keys(0)
    prepare_values(0)
    for t in range(tiles):
        score_tile(0, t)
    for t in range(tiles):
        qt[:, tile_at(t)] = jnp.transpose(qa[tile_at(t), :LANES])
        gt[:, tile_at(t)] = jnp.transpose(ga[tile_at(t), :LANES])
    for d in range(1, REACH + 1):
        forward(2, d).wait_recv()
        forward(0, d).wait_recv()
        prepare_keys(d)
        for t in range(tiles):
            score_tile(d, t)
    for t in range(tiles):
        log_norm_tile(t)

    for d in range(REACH + 1):
        if d > 0:
            forward(1, d).wait_recv()
            prepare_values(d)
        sums = [None] * groups
        for t in range(tiles):
            add_up(sums, d, t, value_tile(d, t))
        for j, g in enumerate(lane_groups(tokens)):
            if d > 0:
                part[1, d, :, g] = sums[j].astype(BF)
            else:
                dvt[:, g] = sums[j]
        if d > 0:
            backward(1, d).start()

    for t in range(tiles):
        delta_feature_tile(t)

    stores = []
    for d in range(REACH, -1, -1):
        sums = [None] * groups
        if d == 0:
            val_total = dvt[...]
            for b in range(REACH, 0, -1):
                backward(1, b).wait_recv()
                val_total = val_total + got[1, b].astype(F32)
            dv_ref[...] = jnp.transpose(val_total).astype(BF)
        for t in range(tiles):
            add_up(sums, d, t, key_tile(d, t))
            if d == 0:
                stores.append(pltpu.make_async_copy(dq_bf.at[tile_at(t)], dq_hbm.at[tile_at(t)], store_sem.at[t]))
                stores[-1].start()
        if d > 0:
            for j, g in enumerate(lane_groups(tokens)):
                part[0, d, :, g] = sums[j].astype(BF)
            backward(0, d).start()

    key_total = jnp.concatenate(sums, axis=1)
    for d in range(REACH, 0, -1):
        backward(0, d).wait_recv()
        key_total = key_total + got[0, d].astype(F32)
    dk_ref[...] = jnp.transpose(key_total).astype(BF)
    for copy in stores:
        copy.wait()
    for d in range(1, REACH + 1):
        for half in range(2):
            forward(half, d).wait_send()
            backward(half, d).wait_send()
        forward(2, d).wait_send()


def finish(dq_in, dk_in, dv_in, dq_out, dk_out, dv_out, sems):
    pairs = ((dq_in, dq_out), (dk_in, dk_out), (dv_in, dv_out))
    copies = [pltpu.make_async_copy(taken, given, sems.at[i]) for i, (taken, given) in enumerate(pairs)]
    for copy in copies:
        copy.start()
    for copy in copies:
        copy.wait()


def local(outer, inner, queries, keys, values, grad_out, doc_ids):
    tokens, heads, width = queries.shape
    rows = tokens * heads
    vmem = pltpu.VMEM
    slots = REACH + 1
    grad_queries, grad_keys, grad_values = pl.pallas_call(
        functools.partial(kernel, outer, inner),
        out_shape=(
            jax.ShapeDtypeStruct((rows, width), BF),
            jax.ShapeDtypeStruct((tokens, width), BF),
            jax.ShapeDtypeStruct((tokens, width), BF),
        ),
        in_specs=[pl.BlockSpec(memory_space=pl.ANY)] * 4 + [pl.BlockSpec(memory_space=vmem)],
        out_specs=(
            pl.BlockSpec(memory_space=pl.ANY),
            pl.BlockSpec(memory_space=vmem),
            pl.BlockSpec(memory_space=vmem),
        ),
        scratch_shapes=[
            vmem((slots, 2 * tokens + 16, width), BF),
            vmem((rows, 2 * width), BF),
            vmem((rows, 2 * width), BF),
            vmem((width, rows), BF),
            vmem((width, rows), BF),
            vmem((slots, 2 * width, tokens), BF),
            vmem((slots, 2 * width, tokens), BF),
            vmem((REACH - 1, rows, tokens), F32),
            vmem((rows, tokens + TILE), F32),
            vmem((rows, width), F32),
            vmem((rows, width), F32),
            vmem((rows, width), F32),
            vmem((width, tokens), F32),
            vmem((2, slots, width, tokens), BF),
            vmem((2, slots, width, tokens), BF),
            vmem((rows, width), BF),
            pltpu.SemaphoreType.DMA((4,)),
            pltpu.SemaphoreType.DMA((tokens // TILE,)),
            pltpu.SemaphoreType.DMA((3, slots)),
            pltpu.SemaphoreType.DMA((3, slots)),
            pltpu.SemaphoreType.DMA((2, slots)),
            pltpu.SemaphoreType.DMA((2, slots)),
        ],
        compiler_params=pltpu.CompilerParams(
            collective_id=0, has_side_effects=True, vmem_limit_bytes=60 * 2**20
        ),
        cost_estimate=pl.CostEstimate(
            flops=12 * rows * 1664 * width, bytes_accessed=8 * rows * width, transcendentals=2 * rows * 1664
        ),
    )(
        queries.reshape(rows, width),
        keys,
        values,
        grad_out.reshape(rows, width),
        doc_ids.reshape(tokens // LANES, LANES),
    )
    grad_queries, grad_keys, grad_values = pl.pallas_call(
        finish,
        out_shape=(
            jax.ShapeDtypeStruct((rows, width), BF),
            jax.ShapeDtypeStruct((tokens, width), BF),
            jax.ShapeDtypeStruct((tokens, width), BF),
        ),
        in_specs=[pl.BlockSpec(memory_space=vmem)] * 3,
        out_specs=[pl.BlockSpec(memory_space=pl.ANY)] * 3,
        scratch_shapes=[pltpu.SemaphoreType.DMA((3,))],
    )(grad_queries, grad_keys, grad_values)
    return grad_queries.reshape(queries.shape), grad_keys, grad_values


def solution(mesh):
    both = ("outer", "inner")
    return jax.shard_map(
        functools.partial(local, mesh.shape["outer"], mesh.shape["inner"]),
        mesh=mesh,
        in_specs=(P(both, None, None), P(both, None), P(both, None), P(both, None, None), P(both)),
        out_specs=(P(both, None, None), P(both, None), P(both, None)),
        check_vma=False,
    )
```
